32 devices in a mesh: dp: 4 (over z), ctx: 4 (over y, x), tensor: 2 (over core).
Axes of the slice: x: 2, y: 2, z: 4, core: 2. Of those that a mesh axis runs over, the one named last changes fastest.
Arguments:
- hidden: bfloat16 [8, 2048, 1024], P('dp', 'ctx'), may hold values from -6 to 6
- out_grad: bfloat16 [8, 2048, 1024], P('dp', 'ctx'), may hold values from -6 to 6
- pre_gain: float32 [2, 1024], replicated, may hold values from 0.5 to 1.5
- gate_inner_weight: bfloat16 [2, 1024, 2, 2048], P(None, 'ctx', None, 'tensor'), may hold values from -0.1875 to 0.1875
- state_maps_weight: bfloat16 [2, 1024, 256], P(None, 'ctx', 'tensor'), may hold values from -0.1875 to 0.1875
- step_size_weight: bfloat16 [2, 1024, 32], P(None, 'ctx', 'tensor'), may hold values from -0.1875 to 0.1875
- conv_x: float32 [2, 4, 2048], P(None, None, 'tensor'), may hold values from -3 to 3
- bias_x: float32 [2, 2048], P(None, 'tensor'), may hold values from -3 to 3
- conv_bc: float32 [2, 4, 256], P(None, None, 'tensor'), may hold values from -3 to 3
- bias_bc: float32 [2, 256], P(None, 'tensor'), may hold values from -3 to 3
- dt_bias: float32 [2, 32], P(None, 'tensor'), may hold values from -7 to -2
- a_log: float32 [2, 32], P(None, 'tensor'), may hold values from 0 to 2.77
- d_skip: float32 [2, 32], P(None, 'tensor'), may hold values from 0.1 to 1.9
- norm_gain: float32 [2, 2048], P(None, 'tensor'), may hold values from 0.5 to 1.5
- output_weight: bfloat16 [2, 2048, 1024], P(None, 'tensor', 'ctx'), may hold values from -0.125 to 0.125
Outputs:
- output: float32 [8, 2048, 1024], P('dp', 'ctx')
- grad_hidden: float32 [8, 2048, 1024], P('dp', 'ctx')
- grad_pre_gain: float32 [2, 1024], replicated
- grad_proj_zx: float32 [2, 1024, 2, 2048], P(None, 'ctx', None, 'tensor')
- grad_proj_bc: float32 [2, 1024, 256], P(None, 'ctx', 'tensor')
- grad_proj_dt: float32 [2, 1024, 32], P(None, 'ctx', 'tensor')
- grad_conv_x: float32 [2, 4, 2048], P(None, None, 'tensor')
- grad_bias_x: float32 [2, 2048], P(None, 'tensor')
- grad_conv_bc: float32 [2, 4, 256], P(None, None, 'tensor')
- grad_bias_bc: float32 [2, 256], P(None, 'tensor')
- grad_dt_bias: float32 [2, 32], P(None, 'tensor')
- grad_a_log: float32 [2, 32], P(None, 'tensor')
- grad_d_skip: float32 [2, 32], P(None, 'tensor')
- grad_norm_gain: float32 [2, 2048], P(None, 'tensor')
- grad_proj_out: float32 [2, 2048, 1024], P(None, 'tensor', 'ctx')
The draws below stay inside these ranges and needn't reach their ends.
All inputs are finite; a program needn't handle non-finite values.
Results may differ from the reference program's by a relative error of at most 0.03.
Values may be sent and summed in bfloat16 or wider, within the bound.
A program may use at most 256 MiB of HBM per device.

```python
import jax
import jax.numpy as jnp
from jax import lax

D = 1024
HEADS = 32
HEAD_DIM = 64
STATE = 128
KCONV = 4
GROUP = 256
LAYERS = 2
DI = 2048
LEN = 2048
NSEQ = 8


def levels(key, extent, cuts, least, high):
    def one(axis_at, parts):
        draws = jax.random.uniform(jax.random.fold_in(jax.random.fold_in(key, 6), axis_at), (parts,), jnp.float32, least / len(cuts), high / len(cuts))
        return jnp.repeat(jnp.exp(draws), extent[axis_at] // parts).reshape((-1,) + (1,) * (len(extent) - axis_at - 1))

    level = one(*cuts[0])
    for cut in cuts[1:]:
        level = level * one(*cut)
    return level


def scatter_about(key, dims, spread, limit, cuts=(), kind=jnp.bfloat16):
    factor_of = levels(key, dims, cuts, -0.22, 0.18) if cuts else 1.0
    values = jax.random.normal(key, dims, jnp.float32) * spread * factor_of
    return jnp.minimum(jnp.maximum(values, -limit), limit).astype(kind)


def setup_inputs(seed: int = 0) -> dict:
    arg_keys = jax.random.split(jax.random.key(seed), 16)
    hidden = scatter_about(arg_keys[0], (NSEQ, LEN, D), 1.0, 6.0, ((0, 4), (1, 4)))
    out_grad = scatter_about(arg_keys[1], (NSEQ, LEN, D), 1.0, 6.0, ((0, 4), (1, 4)))
    pre_gain = jnp.clip(1.0 + 0.1 * jax.random.normal(arg_keys[2], (LAYERS, D), jnp.float32), 0.5, 1.5)
    gate_inner_weight = scatter_about(arg_keys[3], (LAYERS, D, 2, DI), D ** -0.5, 0.1875, ((1, 4), (3, 2)))
    state_maps_weight = scatter_about(arg_keys[4], (LAYERS, D, 2 * STATE), D ** -0.5, 0.1875, ((1, 4), (2, 2)))
    step_size_weight = scatter_about(arg_keys[5], (LAYERS, D, HEADS), D ** -0.5, 0.1875, ((1, 4), (2, 2)))
    conv_x = scatter_about(arg_keys[6], (LAYERS, KCONV, DI), KCONV ** -0.5, 3.0, ((2, 2),), jnp.float32)
    bias_x = scatter_about(arg_keys[7], (LAYERS, DI), 0.5, 3.0, ((1, 2),), jnp.float32)
    conv_bc = scatter_about(arg_keys[8], (LAYERS, KCONV, 2 * STATE), KCONV ** -0.5, 3.0, ((2, 2),), jnp.float32)
    bias_bc = scatter_about(arg_keys[9], (LAYERS, 2 * STATE), 0.5, 3.0, ((1, 2),), jnp.float32)
    dt_bias = jnp.clip(-7.0 + 5.0 * jax.random.uniform(arg_keys[10], (LAYERS, HEADS), jnp.float32) ** levels(arg_keys[10], (LAYERS, HEADS), ((1, 2),), -0.2, 0.2), -7.0, -2.0)
    a_log = jnp.clip(2.77 * jax.random.uniform(arg_keys[11], (LAYERS, HEADS), jnp.float32) ** levels(arg_keys[11], (LAYERS, HEADS), ((1, 2),), -0.2, 0.2), 0.0, 2.77)
    d_skip = jnp.clip(1.0 + 0.18 * jax.random.normal(arg_keys[12], (LAYERS, HEADS), jnp.float32), 0.1, 1.9)
    norm_gain = jnp.clip(1.0 + 0.1 * jax.random.normal(arg_keys[13], (LAYERS, DI), jnp.float32), 0.5, 1.5)
    output_weight = scatter_about(arg_keys[14], (LAYERS, DI, D), DI ** -0.5, 0.125, ((1, 2), (2, 4)))
    return {"hidden": hidden, "out_grad": out_grad, "pre_gain": pre_gain, "gate_inner_weight": gate_inner_weight, "state_maps_weight": state_maps_weight, "step_size_weight": step_size_weight, "conv_x": conv_x, "bias_x": bias_x, "conv_bc": conv_bc, "bias_bc": bias_bc, "dt_bias": dt_bias, "a_log": a_log, "d_skip": d_skip, "norm_gain": norm_gain, "output_weight": output_weight}


epsilon = 1e-05
highest_precision = lax.Precision.HIGHEST

@jax.custom_vjp
def lower_precision(v):
    return lax.optimization_barrier(v.astype(jnp.bfloat16)).astype(jnp.float32)

@jax.custom_vjp
def lower_precision_backward(v):
    return v

def low_keep(v):
    return (lower_precision(v), None)

def low_pass(kept, grad):
    return (grad,)

def back_keep(v):
    return (v, None)

def back_low(kept, grad):
    return (lower_precision(grad),)
lower_precision.defvjp(low_keep, low_pass)
lower_precision_backward.defvjp(back_keep, back_low)

def causal_conv(values, kernel, offset):
    padded = jnp.pad(values, ((0, 0), (KCONV - 1, 0), (0, 0)))
    summed = offset
    for tap_index in range(KCONV):
        summed = summed + kernel[tap_index] * padded[:, tap_index:tap_index + values.shape[1]]
    return summed

def group_step(carried, pieces):
    inputs_x, log_decay, step_size, keys_b, queries_c = pieces
    cumul = jnp.cumsum(log_decay, axis=1)
    scores = lower_precision_backward(jnp.einsum('stn,sun->stu', queries_c, keys_b, precision=highest_precision))
    differ = cumul[:, :, None, :] - cumul[:, None, :, :]
    causal = (jnp.arange(GROUP)[:, None] >= jnp.arange(GROUP)[None, :])[None, :, :, None]
    decay_mask = jnp.where(causal, jnp.exp(jnp.where(causal, differ, 0.0)), 0.0)
    mixing = lower_precision(scores[..., None] * decay_mask * step_size[:, None, :, :])
    within = jnp.einsum('stuh,suhp->sthp', mixing, inputs_x, precision=highest_precision)
    from_state = jnp.einsum('stn,shpn->sthp', queries_c, carried, precision=highest_precision) * jnp.exp(cumul)[..., None]
    weights_end = jnp.exp(cumul[:, -1:, :] - cumul) * step_size
    fresh_state = jnp.einsum('sthp,stn->shpn', inputs_x * weights_end[..., None], keys_b, precision=highest_precision)
    new_state = carried * jnp.exp(cumul[:, -1, :])[:, :, None, None] + fresh_state
    return (new_state, within + from_state)

def scan_ssd(inputs_x, log_decay, step_size, keys_b, queries_c):
    blocks = LEN // GROUP

    def to_blocks(array):
        return jnp.moveaxis(array.reshape((array.shape[0], blocks, GROUP) + array.shape[2:]), 1, 0)
    initial = jnp.zeros((inputs_x.shape[0], HEADS, HEAD_DIM, STATE), jnp.float32)
    last_state, outputs = lax.scan(jax.checkpoint(group_step), initial, (to_blocks(inputs_x), to_blocks(log_decay), to_blocks(step_size), to_blocks(keys_b), to_blocks(queries_c)))
    return jnp.moveaxis(outputs, 0, 1).reshape(inputs_x.shape)

def mixer_layer(stream, pre_gain, gate_inner_weight, state_maps_weight, step_size_weight, conv_x, bias_x, conv_bc, bias_bc, dt_bias, a_log, d_skip, norm_gain, output_weight):
    inv_rms = lax.rsqrt(lax.optimization_barrier(jnp.mean(stream * stream, axis=-1, keepdims=True)) + epsilon)
    normalized_input = lower_precision(stream * inv_rms * pre_gain)
    gate_and_inner = lower_precision_backward(lower_precision(jnp.einsum('mrq,qtn->mrtn', normalized_input, gate_inner_weight, precision=highest_precision)))
    gate_z = gate_and_inner[:, :, 0]
    inner_x = gate_and_inner[:, :, 1]
    state_maps_input = lower_precision_backward(lower_precision(jnp.einsum('crb,bf->crf', normalized_input, state_maps_weight, precision=highest_precision)))
    unbounded_step_size = lower_precision_backward(lower_precision(jnp.einsum('kic,co->kio', normalized_input, step_size_weight, precision=highest_precision)))
    conved_x = lower_precision(jax.nn.silu(causal_conv(inner_x, conv_x, bias_x)))
    conved_bc = lower_precision(jax.nn.silu(causal_conv(state_maps_input, conv_bc, bias_bc)))
    step_size = jax.nn.softplus(unbounded_step_size + dt_bias)
    log_decay = -jnp.exp(a_log) * step_size
    heads_x = conved_x.reshape(conved_x.shape[:2] + (HEADS, HEAD_DIM))
    ssd_out = scan_ssd(heads_x, log_decay, step_size, conved_bc[..., :STATE], conved_bc[..., STATE:])
    ssd_out = lower_precision_backward(ssd_out + d_skip[:, None] * heads_x).reshape(inner_x.shape)
    gated_y = ssd_out * jax.nn.silu(gate_z)
    inv_gate = lax.rsqrt(lax.optimization_barrier(jnp.mean(gated_y * gated_y, axis=-1, keepdims=True)) + epsilon)
    gated_output = lower_precision(gated_y * inv_gate * norm_gain)
    mixer_branch = lower_precision_backward(jnp.einsum('zvo,ok->zvk', gated_output, output_weight, precision=highest_precision))
    return stream + mixer_branch

def reference(hidden, out_grad, pre_gain, gate_inner_weight, state_maps_weight, step_size_weight, conv_x, bias_x, conv_bc, bias_bc, dt_bias, a_log, d_skip, norm_gain, output_weight):
    params = (pre_gain, gate_inner_weight.astype(jnp.float32), state_maps_weight.astype(jnp.float32), step_size_weight.astype(jnp.float32), conv_x, bias_x, conv_bc, bias_bc, dt_bias, a_log, d_skip, norm_gain, output_weight.astype(jnp.float32))

    def forward(stream, weights):
        for layer_index in range(LAYERS):
            stream = mixer_layer(stream, *[member[layer_index] for member in weights])
        return stream
    result, pull_back = jax.vjp(forward, hidden.astype(jnp.float32), params)
    grad_in, grads = pull_back(out_grad.astype(jnp.float32))
    return (result, grad_in, grads[0], grads[1], grads[2], grads[3], grads[4], grads[5], grads[6], grads[7], grads[8], grads[9], grads[10], grads[11], grads[12])
```

```python
import jax
import jax.numpy as jnp
from jax import lax
from jax.experimental import pallas as pl
from jax.experimental.pallas import tpu as pltpu
from jax.sharding import PartitionSpec as P

HEAD_DIM = 64
STATE = 128
KCONV = 4
LAYERS = 2
DI = 2048
PAIR = 128
WIDE = 256
SPAN = 256
HALO = 8

epsilon = 1e-05
highest_precision = lax.Precision.HIGHEST
f32 = jnp.float32
bf16 = jnp.bfloat16


def along(shard, by):
    count = lax.axis_size("ctx")
    pairs = [(i, i + by) for i in range(count) if 0 <= i + by < count]
    return lax.ppermute(shard, "ctx", pairs)


def swap(shard):
    return lax.ppermute(shard, "tensor", [(0, 1), (1, 0)])


def chain(log_total, state, way):
    count = lax.axis_size("ctx")
    sent = state.astype(bf16)
    logs = jnp.zeros_like(log_total)
    total = jnp.zeros(state.shape, f32)
    for hop in range(1, count):
        part = along(sent, way * hop).astype(f32)
        factor = jnp.repeat(jnp.exp(logs), HEAD_DIM, axis=1)[:, :, None]
        total = total + factor * part
        if hop < count - 1:
            logs = logs + along(log_total, way * hop)
    return total


def prenorm(stream, gain):
    inv_rms = lax.rsqrt(jnp.mean(stream * stream, axis=-1, keepdims=True) + epsilon)
    return stream * inv_rms * gain


def conv_act(padded, kernel, offset):
    length = padded.shape[1] - KCONV + 1
    summed = offset
    for tap_index in range(KCONV):
        summed = summed + kernel[tap_index] * padded[:, tap_index : tap_index + length]
    return jax.nn.silu(summed)


def dot(a, b, over):
    return lax.dot_general(a, b, (((over[0],), (over[1],)), ((), ())), preferred_element_type=f32)


def selector(place, heads, width):
    row = lax.broadcasted_iota(jnp.int32, (heads, width), 0)
    lane = lax.broadcasted_iota(jnp.int32, (heads, width), 1)
    head = place * (width // HEAD_DIM) + lax.shift_right_logical(lane, 6)
    return jnp.where(row == head, 1.0, 0.0).astype(bf16)


def spread(values, select, terms):
    rest, total = values, None
    for term in range(terms):
        piece = rest.astype(bf16)
        part = dot(piece, select, (1, 0))
        total = part if total is None else total + part
        rest = rest - piece.astype(f32)
    return total


def gathered(values, select):
    high = values.astype(bf16)
    low = (values - high.astype(f32)).astype(bf16)
    return dot(high, select, (1, 1)) + dot(low, select, (1, 1))


def head_lanes(values, member):
    lane = lax.broadcasted_iota(jnp.int32, values.shape, 1)
    return jnp.where(lax.shift_right_logical(lane, 6) == member, values, jnp.zeros_like(values))


def decay_of(wide_log, row_log, member, start):
    stop = start + SPAN
    column = wide_log[start:stop, member * HEAD_DIM : member * HEAD_DIM + 1]
    differ = column - row_log[member : member + 1, :stop]
    token = lax.broadcasted_iota(jnp.int32, differ.shape, 0) + start
    other = lax.broadcasted_iota(jnp.int32, differ.shape, 1)
    return jnp.where(other <= token, jnp.exp(differ), 0.0)


def sigmoid(v):
    return 1.0 / (1.0 + jnp.exp(-v))


def convolve(pad_ref, values, rim, taps, offset):
    length = values.shape[0]
    pad_ref[0:HALO, :] = rim
    pad_ref[HALO : HALO + length, :] = values
    summed = offset
    for tap in range(KCONV):
        begin = HALO - KCONV + 1 + tap
        summed = summed + taps[tap : tap + 1] * pad_ref[begin : begin + length, :]
    return summed


def state_kernel(inner_ref, rim_ref, taps_ref, bias_ref, log_ref, step_ref, keys_ref, x_ref, state_ref, pad_ref):
    select = selector(pl.program_id(1), log_ref.shape[2], PAIR)
    length = inner_ref.shape[0]
    pre = convolve(pad_ref, inner_ref[...].astype(f32), rim_ref[0], taps_ref[...], bias_ref[...])
    x = (pre * sigmoid(pre)).astype(bf16)
    x_ref[...] = x
    wide_log = spread(log_ref[0], select, 3)
    wide_step = spread(step_ref[0], select, 2)
    weighted = x.astype(f32) * wide_step * jnp.exp(wide_log[length - 1 :] - wide_log)
    state_ref[0] = dot(weighted.astype(bf16), keys_ref[...], (0, 0)).astype(bf16)


def output_kernel(x_ref, gate_ref, keys_ref, queries_ref, log_ref, row_ref, step_ref, state_ref, skip_ref, gain_ref, ssd_ref, out_ref, square_ref, score_ref):
    place = pl.program_id(1)
    select = selector(place, log_ref.shape[2], PAIR)
    length = x_ref.shape[0]

    @pl.when(place == 0)
    def _():
        score_ref[...] = dot(queries_ref[...], keys_ref[...], (1, 1))
        square_ref[...] = jnp.zeros_like(square_ref)

    x = x_ref[...].astype(f32)
    wide_log = spread(log_ref[0], select, 3)
    wide_step = spread(step_ref[0], select, 2)
    scaled = (x * wide_step).astype(bf16)
    split = [head_lanes(scaled, member) for member in range(2)]
    rows = []
    for start in range(0, length, SPAN):
        stop = start + SPAN
        total = None
        for member in range(2):
            decay = decay_of(wide_log, row_ref[0, 0], member, start)
            mixing = (score_ref[start:stop, :stop] * decay).astype(bf16)
            part = dot(mixing, split[member][:stop], (1, 0))
            total = part if total is None else total + part
        rows.append(total)
    within = jnp.concatenate(rows, axis=0)
    carried = jnp.exp(wide_log) * dot(queries_ref[...], state_ref[0], (1, 1))
    ssd = within + carried + skip_ref[...] * x
    gate = gate_ref[...].astype(f32)
    gated = ssd * gate * sigmoid(gate)
    ssd_ref[...] = ssd.astype(bf16)
    out_ref[...] = (gated * gain_ref[...]).astype(bf16)
    square_ref[...] += gated * gated


def gate_kernel(grad_ref, weight_ref, gate_ref, ssd_ref, gain_ref, inv_ref, cross_ref, log_ref, queries_ref, d_ssd_ref, d_gate_ref, norm_ref, state_ref):
    select = selector(pl.program_id(1), log_ref.shape[2], WIDE)
    d_out = dot(grad_ref[...], weight_ref[...], (1, 0))
    gate = gate_ref[...].astype(f32)
    ssd = ssd_ref[...].astype(f32)
    sig = sigmoid(gate)
    silu = gate * sig
    gated = ssd * silu
    inv = inv_ref[...]
    norm_ref[0] = jnp.sum(d_out * gated * inv, axis=0, keepdims=True)
    d_gated = inv * (d_out * gain_ref[...]) - gated * cross_ref[...]
    d_gate_ref[...] = (d_gated * ssd * sig * (1.0 + gate * (1.0 - sig))).astype(bf16)
    d_ssd = (d_gated * silu).astype(bf16)
    d_ssd_ref[...] = d_ssd
    wide_log = spread(log_ref[0], select, 3)
    weighted = (d_ssd.astype(f32) * jnp.exp(wide_log)).astype(bf16)
    state_ref[0] = dot(weighted, queries_ref[...], (0, 0)).astype(bf16)


def grad_kernel(
    x_ref, inner_ref, rim_ref, taps_ref, bias_ref, keys_ref, queries_ref, log_ref, row_ref, step_ref, state_ref, lam_ref, skip_ref, d_ssd_ref,
    d_inner_ref, d_rim_ref, d_taps_ref, d_bias_ref, d_skip_ref, d_keys_ref, d_queries_ref, d_log_ref, d_end_ref, d_step_ref,
    score_ref, d_score_ref, pad_ref, tail_ref, d_scaled_ref,
):
    place = pl.program_id(1)
    select = selector(place, log_ref.shape[2], PAIR)
    length = x_ref.shape[0]
    keys, queries = keys_ref[...], queries_ref[...]

    @pl.when(place == 0)
    def _():
        score_ref[...] = dot(queries, keys, (1, 1))
        for ref in (d_score_ref, d_keys_ref, d_queries_ref, d_log_ref, d_end_ref, d_step_ref):
            ref[...] = jnp.zeros_like(ref)

    x = x_ref[...].astype(f32)
    d_ssd = d_ssd_ref[...]
    d_ssd_f = d_ssd.astype(f32)
    wide_log = spread(log_ref[0], select, 3)
    wide_step = spread(step_ref[0], select, 2)
    scaled = (x * wide_step).astype(bf16)
    scaled_f = scaled.astype(f32)
    split = [head_lanes(scaled, member) for member in range(2)]
    d_split = [head_lanes(d_ssd, member) for member in range(2)]
    d_scaled_ref[...] = jnp.zeros_like(d_scaled_ref)
    rows = []
    for start in range(0, length, SPAN):
        stop = start + SPAN
        total, back, d_score = None, None, None
        for member in range(2):
            decay = decay_of(wide_log, row_ref[0, 0], member, start)
            mixing = (score_ref[start:stop, :stop] * decay).astype(bf16)
            part = dot(mixing, split[member][:stop], (1, 0))
            grad = dot(mixing, d_split[member][start:stop], (0, 0))
            d_part = dot(d_ssd[start:stop], split[member][:stop], (1, 1)) * decay
            total = part if total is None else total + part
            back = grad if back is None else back + grad
            d_score = d_part if d_score is None else d_score + d_part
        rows.append(total)
        d_scaled_ref[:stop, :] += back
        d_score_ref[start:stop, :stop] += d_score
    grown = jnp.exp(wide_log)
    fading = jnp.exp(wide_log[length - 1 :] - wide_log)
    read = jnp.concatenate(rows, axis=0) + grown * dot(queries, state_ref[0], (1, 1))
    d_within = d_scaled_ref[...]
    d_state = fading * dot(keys, lam_ref[0], (1, 1))
    d_scaled = d_within + d_state
    d_log_ref[0] += gathered(d_ssd_f * read - scaled_f * d_within, select)
    d_end_ref[0] += gathered(scaled_f * d_state, select)
    d_step_ref[0] += gathered(x * d_scaled, select)
    d_skip_ref[0] = jnp.sum(d_ssd_f * x, axis=0, keepdims=True)
    d_keys_ref[...] += dot((scaled_f * fading).astype(bf16), lam_ref[0], (1, 0))
    d_queries_ref[...] += dot((d_ssd_f * grown).astype(bf16), state_ref[0], (1, 0))

    taps = taps_ref[...]
    pre = convolve(pad_ref, inner_ref[...].astype(f32), rim_ref[0], taps, bias_ref[...])
    sig = sigmoid(pre)
    d_pre = (wide_step * d_scaled + skip_ref[...] * d_ssd_f) * sig * (1.0 + pre * (1.0 - sig))
    d_bias_ref[0] = jnp.sum(d_pre, axis=0, keepdims=True)
    tail_ref[0:HALO, :] = jnp.zeros((HALO, PAIR), f32)
    tail_ref[HALO : HALO + length, :] = d_pre
    tail_ref[HALO + length :, :] = jnp.zeros((HALO, PAIR), f32)
    inner = None
    rim = None
    for tap in range(KCONV):
        begin = HALO - KCONV + 1 + tap
        d_taps_ref[0, tap : tap + 1, :] = jnp.sum(d_pre * pad_ref[begin : begin + length, :], axis=0, keepdims=True)
        ahead = KCONV - 1 - tap
        part = taps[tap : tap + 1] * tail_ref[HALO + ahead : HALO + ahead + length, :]
        edge = taps[tap : tap + 1] * tail_ref[ahead : ahead + HALO, :]
        inner = part if inner is None else inner + part
        rim = edge if rim is None else rim + edge
    d_inner_ref[...] = inner.astype(bf16)
    d_rim_ref[0] = rim

    @pl.when(place == pl.num_programs(1) - 1)
    def _():
        d_scores = d_score_ref[...].astype(bf16)
        d_queries_ref[...] += dot(d_scores, keys, (1, 0))
        d_keys_ref[...] += dot(d_scores, queries, (0, 0))


params = pltpu.CompilerParams(vmem_limit_bytes=48 * 1024 * 1024)


def body(
    hidden,
    out_grad,
    pre_gain,
    gate_inner_weight,
    state_maps_weight,
    step_size_weight,
    conv_x,
    bias_x,
    conv_bc,
    bias_bc,
    dt_bias,
    a_log,
    d_skip,
    norm_gain,
    output_weight,
):
    seqs, length, width = hidden.shape
    rows = seqs * length
    depth = gate_inner_weight.shape[1]
    inner = gate_inner_weight.shape[3]
    heads = inner // HEAD_DIM
    pairs = inner // PAIR
    maps = state_maps_weight.shape[2]
    first_maps, first_dt = 2 * inner, 2 * inner + maps
    columns = first_dt + 128
    core = lax.axis_index("tensor")
    lower = (jnp.arange(length)[:, None] >= jnp.arange(length)[None, :]).astype(f32)
    strict = (jnp.arange(length)[:, None] > jnp.arange(length)[None, :]).astype(f32)

    def run_sum(tri, values, order):
        return jnp.einsum(order, tri, values, precision=highest_precision)

    def cols(offset=0, wide=PAIR):
        return pl.BlockSpec((length, wide), lambda s, j: (s, j + offset))

    per_seq = pl.BlockSpec((length, STATE), lambda s, j: (s, 0))
    head_spec = pl.BlockSpec((1, length, heads), lambda s, j: (s, 0, 0))
    row_spec = pl.BlockSpec((1, 1, 2, length), lambda s, j: (s, j, 0, 0))
    state_spec = pl.BlockSpec((1, PAIR, STATE), lambda s, j: (s, j, 0))
    rim_spec = pl.BlockSpec((1, HALO, PAIR), lambda s, j: (s, 0, j))
    taps_spec = pl.BlockSpec((KCONV, PAIR), lambda s, j: (0, j))
    lane_spec = pl.BlockSpec((1, PAIR), lambda s, j: (0, j))
    sum_spec = pl.BlockSpec((1, 1, PAIR), lambda s, j: (s, 0, j))

    def shape(dims, kind):
        return jax.ShapeDtypeStruct(dims, kind)

    def shards(l):
        into = jnp.concatenate(
            [
                gate_inner_weight[l].reshape(depth, 2 * inner),
                state_maps_weight[l],
                jnp.pad(step_size_weight[l], ((0, 0), (0, 128 - heads))),
            ],
            axis=1,
        )
        return into, output_weight[l].T

    def gather(v):
        return lax.all_gather(v, "ctx", axis=0, tiled=True)

    stream = hidden.astype(f32).reshape(rows, width)
    kept = []
    for l in range(LAYERS):
        into, out_t = shards(l)
        if l > 0:
            kept[l - 1][0], into = lax.optimization_barrier((kept[l - 1][0], into))
        full_in = gather(into)
        full_in, out_t = lax.optimization_barrier((full_in, out_t))
        full_out = gather(out_t)
        normed_f, norm_pull = jax.vjp(prenorm, stream, pre_gain[l])
        normed = normed_f.astype(bf16)
        proj = jnp.dot(normed, full_in, preferred_element_type=f32).astype(bf16)
        rims = along(proj.reshape(seqs, length, columns)[:, length - KCONV + 1 :, inner:first_dt], 1).astype(f32)
        rim_x = jnp.pad(rims[:, :, :inner], ((0, 0), (HALO - KCONV + 1, 0), (0, 0)))
        bc = proj[:, first_maps:first_dt].astype(f32).reshape(seqs, length, maps)
        padded_bc = jnp.concatenate([rims[:, :, inner:], bc], axis=1)
        act_bc, pull_bc = jax.vjp(conv_act, padded_bc, conv_bc[l], bias_bc[l])
        own = act_bc.astype(bf16).reshape(rows, maps)
        other = swap(own)
        keys = jnp.where(core == 0, own, other)
        queries = jnp.where(core == 0, other, own)
        raw = proj[:, first_dt : first_dt + heads].astype(f32).reshape(seqs, length, heads)
        step = jax.nn.softplus(raw + dt_bias[l])
        rate = jnp.exp(a_log[l])
        log = run_sum(lower, -rate * step, "tu,suh->sth")
        row_log = jnp.swapaxes(log, 1, 2).reshape(seqs, pairs, 2, length)
        log_total = log[:, -1]
        taps, offset = conv_x[l], bias_x[l][None]
        x, state = pl.pallas_call(
            state_kernel,
            grid=(seqs, pairs),
            in_specs=[cols(pairs), rim_spec, taps_spec, lane_spec, head_spec, head_spec, per_seq],
            out_specs=[cols(), state_spec],
            out_shape=[shape((rows, inner), bf16), shape((seqs, inner, STATE), bf16)],
            scratch_shapes=[pltpu.VMEM((HALO + length, PAIR), f32)],
            compiler_params=params,
        )(proj, rim_x, taps, offset, log, step, keys)
        state_in = chain(log_total, state, 1).astype(bf16)
        skip = jnp.repeat(d_skip[l], HEAD_DIM)[None]
        gain = norm_gain[l][None]
        ssd, gated, square = pl.pallas_call(
            output_kernel,
            grid=(seqs, pairs),
            in_specs=[cols(), cols(), per_seq, per_seq, head_spec, row_spec, head_spec, state_spec, lane_spec, lane_spec],
            out_specs=[cols(), cols(), per_seq],
            out_shape=[shape((rows, inner), bf16), shape((rows, inner), bf16), shape((rows, PAIR), f32)],
            scratch_shapes=[pltpu.VMEM((length, length), f32)],
            compiler_params=params,
        )(x, proj, keys, queries, log, row_log, step, state_in, skip, gain)
        square = jnp.sum(square, axis=1)
        square = square + swap(square)
        inv_rms = lax.rsqrt(square / DI + epsilon)[:, None]
        part = dot(gated, full_out, (1, 1)).astype(bf16)
        mixed = part.astype(f32) + swap(part).astype(f32)
        kept.append(
            [full_in, full_out, norm_pull, normed, proj, rim_x, pull_bc, keys, queries, raw, step, rate, log, row_log,
             log_total, x, state_in, skip, gain, ssd, gated, inv_rms, mixed]
        )
        stream = stream + mixed * inv_rms
    output = stream.reshape(seqs, length, width)

    grad = out_grad.astype(f32).reshape(rows, width)
    sums = [None] * LAYERS
    small = [None] * LAYERS
    for l in reversed(range(LAYERS)):
        (full_in, full_out, norm_pull, normed, proj, rim_x, pull_bc, keys, queries, raw, step, rate, log, row_log,
         log_total, x, state_in, skip, gain, ssd, gated, inv_rms, mixed) = kept[l]
        taps, offset = conv_x[l], bias_x[l][None]
        grad_b = grad.astype(bf16)
        cross = jnp.sum(grad_b.astype(f32) * mixed, axis=1, keepdims=True) * (inv_rms * inv_rms * inv_rms) / DI
        blocks = inner // WIDE
        wide_lane = pl.BlockSpec((1, WIDE), lambda s, j: (0, j))
        token_spec = pl.BlockSpec((length, 1), lambda s, j: (s, 0))
        d_ssd, d_gate, grad_norm, d_state = pl.pallas_call(
            gate_kernel,
            grid=(seqs, blocks),
            in_specs=[
                pl.BlockSpec((length, width), lambda s, j: (s, 0)),
                pl.BlockSpec((width, WIDE), lambda s, j: (0, j)),
                cols(0, WIDE), cols(0, WIDE), wide_lane, token_spec, token_spec, head_spec, per_seq,
            ],
            out_specs=[
                cols(0, WIDE), cols(0, WIDE),
                pl.BlockSpec((1, 1, WIDE), lambda s, j: (s, 0, j)),
                pl.BlockSpec((1, WIDE, STATE), lambda s, j: (s, j, 0)),
            ],
            out_shape=[
                shape((rows, inner), bf16), shape((rows, inner), bf16),
                shape((seqs, 1, inner), f32), shape((seqs, inner, STATE), bf16),
            ],
            compiler_params=params,
        )(grad_b, full_out, proj, ssd, gain, inv_rms, cross, log, queries)
        lam = chain(log_total, d_state, -1)
        through = jnp.sum((lam * state_in.astype(f32)).reshape(seqs, heads, HEAD_DIM * STATE), axis=2) * jnp.exp(log_total)
        grad_out = dot((grad_b.astype(f32) * inv_rms).astype(bf16), gated, (0, 0)).astype(bf16)
        out_shard = lax.psum_scatter(grad_out, "ctx", scatter_dimension=0, tiled=True)
        (d_inner, d_rim, d_taps, d_offset, skip_sum, d_keys, d_queries, d_log, d_end, d_step) = pl.pallas_call(
            grad_kernel,
            grid=(seqs, pairs),
            in_specs=[
                cols(), cols(pairs), rim_spec, taps_spec, lane_spec, per_seq, per_seq, head_spec, row_spec, head_spec,
                state_spec, state_spec, lane_spec, cols(),
            ],
            out_specs=[
                cols(), rim_spec, pl.BlockSpec((1, KCONV, PAIR), lambda s, j: (s, 0, j)), sum_spec, sum_spec,
                per_seq, per_seq, head_spec, head_spec, head_spec,
            ],
            out_shape=[
                shape((rows, inner), bf16), shape((seqs, HALO, inner), f32), shape((seqs, KCONV, inner), f32),
                shape((seqs, 1, inner), f32), shape((seqs, 1, inner), f32),
                shape((rows, STATE), f32), shape((rows, STATE), f32),
            ]
            + [shape((seqs, length, heads), f32)] * 3,
            scratch_shapes=[
                pltpu.VMEM((length, length), f32),
                pltpu.VMEM((length, length), f32),
                pltpu.VMEM((HALO + length, PAIR), f32),
                pltpu.VMEM((2 * HALO + length, PAIR), f32),
                pltpu.VMEM((length, PAIR), f32),
            ],
            compiler_params=params,
        )(x, proj, rim_x, taps, offset, keys, queries, log, row_log, step, state_in, lam.astype(bf16), skip, d_ssd)
        theirs = swap(jnp.where(core == 0, d_queries, d_keys).astype(bf16)).astype(f32)
        d_own = jnp.where(core == 0, d_keys, d_queries) + theirs
        d_pad_bc, grad_conv_bc, grad_bias_bc = pull_bc(d_own.reshape(seqs, length, maps))
        edge = along(
            jnp.concatenate([d_rim[:, HALO - KCONV + 1 :], d_pad_bc[:, : KCONV - 1]], axis=2), -1
        )
        d_inner = d_inner.reshape(seqs, length, inner)
        d_tail = (d_inner[:, length - KCONV + 1 :].astype(f32) + edge[:, :, :inner]).astype(bf16)
        d_inner = lax.dynamic_update_slice(d_inner, d_tail, (0, length - KCONV + 1, 0)).reshape(rows, inner)
        d_bc = d_pad_bc[:, KCONV - 1 :].at[:, length - KCONV + 1 :].add(edge[:, :, inner:])
        d_decay = (
            run_sum(lower, d_log, "ut,suh->sth")
            + run_sum(strict, d_end, "tu,suh->sth")
            + through[:, None, :]
        )
        grad_rate = jnp.sum(d_decay * (-rate * step), axis=(0, 1))
        d_raw = (d_step - rate * d_decay) * jax.nn.sigmoid(raw + dt_bias[l])
        grad_dt = jnp.sum(d_raw, axis=(0, 1))
        d_proj = jnp.concatenate(
            [
                d_gate,
                d_inner,
                d_bc.reshape(rows, maps).astype(bf16),
                jnp.pad(d_raw.reshape(rows, heads).astype(bf16), ((0, 0), (0, 128 - heads))),
            ],
            axis=1,
        )
        part = dot(d_proj, full_in, (1, 1)).astype(bf16)
        d_normed = part.astype(f32) + swap(part).astype(f32)
        if l + 1 < LAYERS:
            normed, sums[l + 1] = lax.optimization_barrier((normed, sums[l + 1]))
        grad_in = dot(normed, d_proj, (0, 0)).astype(bf16)
        in_shard = lax.psum_scatter(grad_in, "ctx", scatter_dimension=0, tiled=True)
        d_stream, grad_pre = norm_pull(d_normed)
        grad = grad + d_stream
        sums[l] = (lax.psum(in_shard, "dp"), lax.psum(out_shard, "dp"))
        small[l] = (
            grad_pre,
            jnp.sum(d_taps, axis=0),
            jnp.sum(d_offset, axis=(0, 1)),
            grad_conv_bc,
            grad_bias_bc,
            grad_dt,
            grad_rate,
            jnp.sum(skip_sum.reshape(seqs, heads, HEAD_DIM), axis=(0, 2)),
            jnp.sum(grad_norm, axis=(0, 1)),
        )
    big = [
        (
            in_sum[:, :first_maps].reshape(depth, 2, inner).astype(f32),
            in_sum[:, first_maps:first_dt].astype(f32),
            in_sum[:, first_dt : first_dt + heads].astype(f32),
            out_sum.T.astype(f32),
        )
        for in_sum, out_sum in sums
    ]
    flat = jnp.concatenate([v.reshape(-1) for l in range(LAYERS) for v in small[l]])
    flat = lax.psum(flat, ("dp", "ctx"))
    summed = []
    at = 0
    for l in range(LAYERS):
        row = []
        for v in small[l]:
            row.append(flat[at : at + v.size].reshape(v.shape))
            at += v.size
        summed.append(row)
    s = [jnp.stack([summed[l][m] for l in range(LAYERS)]) for m in range(9)]
    b = [jnp.stack([big[l][m] for l in range(LAYERS)]) for m in range(4)]
    grad_hidden = grad.reshape(seqs, length, width)
    return (output, grad_hidden, s[0], b[0], b[1], b[2], s[1], s[2], s[3], s[4], s[5], s[6], s[7], s[8], b[3])


def solution(mesh):
    return jax.shard_map(
        body,
        mesh=mesh,
        in_specs=(
            P("dp", "ctx", None),
            P("dp", "ctx", None),
            P(),
            P(None, "ctx", None, "tensor"),
            P(None, "ctx", "tensor"),
            P(None, "ctx", "tensor"),
            P(None, None, "tensor"),
            P(None, "tensor"),
            P(None, None, "tensor"),
            P(None, "tensor"),
            P(None, "tensor"),
            P(None, "tensor"),
            P(None, "tensor"),
            P(None, "tensor"),
            P(None, "tensor", "ctx"),
        ),
        out_specs=(
            P("dp", "ctx", None),
            P("dp", "ctx", None),
            P(),
            P(None, "ctx", None, "tensor"),
            P(None, "ctx", "tensor"),
            P(None, "ctx", "tensor"),
            P(None, None, "tensor"),
            P(None, "tensor"),
            P(None, None, "tensor"),
            P(None, "tensor"),
            P(None, "tensor"),
            P(None, "tensor"),
            P(None, "tensor"),
            P(None, "tensor"),
            P(None, "tensor", "ctx"),
        ),
        check_vma=False,
    )
```
